256 devices in a mesh: tm: 16 (over y_lo, x, core), chan: 16 (over z, y_hi).
Axes of the slice: x: 4, y: 4 (y_hi: 2, y_lo: 2; y = y_hi * 2 + y_lo), z: 8, core: 2. Of those that a mesh axis runs over, the one named last changes fastest.
Arguments:
- visibility: float32 [2, 2048, 128, 512], P(None, None, 'tm', 'chan'), may hold values from -8 to 8
- groups: int32 [2048], replicated, may hold values from 0 to 63
- flags: int32 [2048, 512], P(None, 'chan'), may hold values 0 or 1
- fringe: bfloat16 [2, 64, 128, 128], P(None, 'tm'), may hold values from -0.375 to 0.375
- delay: bfloat16 [8, 512, 512], P(None, 'chan'), may hold values from -0.25 to 0.25
Outputs:
- filtered: float32 [2, 2048, 128, 512], P(None, ('tm', 'chan'))
The draws below stay inside these ranges and needn't reach their ends.
All inputs are finite; a program needn't handle non-finite values. No bound on the sum of `flags` on one device may be relied on, other than what follows from the above.
Results may differ from the reference program's by a relative error of at most 0.0003.
Values may be sent and summed in bfloat16 or wider, within the bound.
No kernel may reach another device: no remote copies, remote signals or barrier semaphores. Data moves between devices by JAX's collectives and lax.ppermute only.
A program may use at most 128 MiB of HBM per device.

```python
import jax
import jax.numpy as jnp
from jax import lax

NT = 128
NF = 512
G = 64
DG = 8
NB = 2048


def with_ends(result, stream_key, low, largest):
    dims = result.shape
    index_at = [jax.random.randint(jax.random.fold_in(stream_key, axis), (), 0, dims[axis]) for axis in range(len(dims))]
    result = result.at[tuple(index_at)].set(low)
    longest = dims.index(max(dims))
    index_at[longest] = (index_at[longest] + 1) % dims[longest]
    return result.at[tuple(index_at)].set(largest)


def block_levels(stream_key, extent, cuts, low, top_value):
    factor_of = 1.0
    for position, blocks in cuts:
        steps = jax.random.uniform(jax.random.fold_in(jax.random.fold_in(stream_key, 6), position), (blocks,), jnp.float32, low / len(cuts), top_value / len(cuts))
        factor_of = factor_of * jnp.repeat(jnp.exp(steps), extent[position] // blocks).reshape((-1,) + (1,) * (len(extent) - 1 - position))
    return factor_of


def bell_draw(stream_key, dims, width, limit, cuts=(), kind=jnp.bfloat16):
    loudness = block_levels(stream_key, dims, cuts, -0.22, 0.18) if cuts else 1.0
    drawn = jax.random.normal(stream_key, dims, jnp.float32) * width * loudness
    return jnp.minimum(jnp.maximum(drawn, -limit), limit).astype(kind)


def setup_inputs(seed: int = 0) -> dict:
    key_list = jax.random.split(jax.random.key(seed), 6)
    return {
        "visibility": bell_draw(key_list[0], (2, NB, NT, NF), 1.0, 8.0, ((2, 16), (3, 16)), jnp.float32),
        "groups": with_ends(jax.random.randint(key_list[1], (NB,), 0, G), jax.random.fold_in(key_list[1], 1), 0, G - 1).astype(jnp.int32),
        "flags": with_ends((jax.random.randint(key_list[2], (NB, NF), 0, 8) < 7).astype(jnp.int32), jax.random.fold_in(key_list[2], 1), 0, 1),
        "fringe": bell_draw(key_list[3], (2, G, NT, NT), (2 * NT) ** -0.5, 0.375, ((1, 16),)),
        "delay": bell_draw(key_list[4], (DG, NF, NF), NF ** -0.5, 0.25, ((1, 16),)),
    }


def fringe_apply(data, mats):
    high = lax.Precision.HIGHEST
    real_part = jnp.einsum("btk,bkf->btf", mats[0], data[0], precision=high) - jnp.einsum("btk,bkf->btf", mats[1], data[1], precision=high)
    imag_part = jnp.einsum("btk,bkf->btf", mats[0], data[1], precision=high) + jnp.einsum("btk,bkf->btf", mats[1], data[0], precision=high)
    return jnp.stack([real_part, imag_part])


def reference(visibility, groups, flags, fringe, delay):
    block = 32
    spread = G // DG
    starts = jnp.arange(NB // block, dtype=jnp.int32) * block

    def one_block(start):
        data = lax.dynamic_slice_in_dim(visibility, start, block, 1)
        keep = lax.dynamic_slice_in_dim(flags, start, block, 0).astype(jnp.float32)
        chosen = lax.dynamic_slice_in_dim(groups, start, block, 0)
        masked = data * keep[None, :, None, :]
        mats = jnp.take(fringe, chosen, axis=1).astype(jnp.float32)
        rated = fringe_apply(masked, mats)
        picked = jnp.take(delay, chosen // spread, axis=0).astype(jnp.float32)
        return jnp.einsum("bfk,pbtk->pbtf", picked, rated, precision=lax.Precision.HIGHEST)

    stacked = lax.map(one_block, starts)
    stacked = jnp.moveaxis(stacked, 1, 0)
    return stacked.reshape(2, NB, NT, NF)
```

```python
import functools

import jax
import jax.numpy as jnp
from jax import lax
from jax.experimental import pallas as pl
from jax.experimental.pallas import tpu as pltpu
from jax.sharding import PartitionSpec as P

LANES = 128
SUB = 8
FULL = 32760.0
MIDDLE = 32768.0
VMEM = 40 * 1024 * 1024


def pack_kernel(vis_ref, flag_ref, out_ref, rows):
    for tile in range(vis_ref.shape[3] // LANES):
        lanes = pl.ds(tile * LANES, LANES)
        keep = flag_ref[:, lanes].astype(jnp.float32)
        masked = vis_ref[:, :, :, lanes] * keep[None, None]
        loudest = jnp.max(jnp.abs(masked), axis=(0, 1, 2), keepdims=True)
        level = jnp.ceil(jnp.log2(jnp.maximum(loudest, 1e-30)) * 4.0)
        factor = FULL / jnp.exp2(level * 0.25)
        coded = (masked * factor + (MIDDLE + 0.5)).astype(jnp.int32)
        words = coded[0] | (coded[1] << 16)
        level_row = level.reshape(1, LANES).astype(jnp.int32)
        times, chans = words.shape[0], words.shape[1]
        fold = LANES // chans
        for part in range(times // fold):
            turned = words[part * fold : (part + 1) * fold].reshape(LANES, LANES).T
            for owner in range(LANES // SUB):
                place = (tile * (LANES // SUB) + owner) * rows + part * SUB
                out_ref[place : place + SUB, :] = turned[owner * SUB : (owner + 1) * SUB]
        for owner in range(LANES // SUB):
            place = (tile * (LANES // SUB) + owner) * rows + rows - 1
            out_ref[place : place + 1, :] = level_row


def select_kernel(groups_ref, place_ref, table_ref, out_ref):
    owners, each = out_ref.shape[0], out_ref.shape[1]
    chan_count = groups_ref.shape[0] // (owners * each)

    def step(n, carry):
        owner = n // each
        slot = n % each
        group = groups_ref[(owner * chan_count + place_ref[1]) * each + slot]
        out_ref[owner, slot] = table_ref[group]
        return carry

    lax.fori_loop(0, owners * each, step, 0, unroll=8)


def filter_kernel(
    groups_ref, place_ref, words_ref, fringe_ref, delay_ref, out_ref, levels, samples, *, rows
):
    baseline = pl.program_id(0)
    blocks = words_ref.shape[0]
    chan_count = words_ref.shape[1] // rows
    quads = chan_count // 4
    times = rows - 1

    @pl.when(baseline == 0)
    def unpack():
        lane = lax.broadcasted_iota(jnp.int32, (SUB, LANES), 1)
        low_half = lane < 64
        even_group = (lane & 32) == 0
        group = lane // 32
        level_rows = [
            words_ref[block, source * rows + rows - 1 : source * rows + rows, :]
            for block in range(blocks)
            for source in range(chan_count)
        ]
        level_all = jnp.concatenate(level_rows, axis=0).astype(jnp.float32)
        scale_all = jnp.exp2(level_all * 0.25) * (1.0 / FULL)
        levels[...] = scale_all.T
        own = levels[pl.ds(pl.multiple_of(place_ref[1] * SUB, SUB), SUB), :]
        for block in range(blocks):
            for quad in range(quads):
                first = block * chan_count + quad * 4
                scale = jnp.broadcast_to(own[:, first : first + 1], (SUB, LANES))
                for member in range(1, 4):
                    other = jnp.broadcast_to(own[:, first + member : first + member + 1], (SUB, LANES))
                    scale = jnp.where(group == member, other, scale)
                offset = scale * -MIDDLE
                for half in range(times // SUB):
                    v = [
                        words_ref[block, pl.ds((quad * 4 + member) * rows + half * SUB, SUB), :]
                        for member in range(4)
                    ]
                    r = [pltpu.roll(x, 64, 1) for x in v]
                    a0 = jnp.where(low_half, v[0], r[2])
                    a2 = jnp.where(low_half, r[0], v[2])
                    a1 = jnp.where(low_half, v[1], r[3])
                    a3 = jnp.where(low_half, r[1], v[3])
                    turned = (
                        jnp.where(even_group, a0, pltpu.roll(a1, 32, 1)),
                        jnp.where(even_group, pltpu.roll(a0, 96, 1), a1),
                        jnp.where(even_group, a2, pltpu.roll(a3, 32, 1)),
                        jnp.where(even_group, pltpu.roll(a2, 96, 1), a3),
                    )
                    for step, word in enumerate(turned):
                        at = (block * 8 + half * 4 + step) * SUB
                        real = (word & 0xFFFF).astype(jnp.float32) * scale + offset
                        imag = lax.shift_right_logical(word, 16).astype(jnp.float32) * scale + offset
                        samples[0, quad, at : at + SUB, :] = real
                        samples[1, quad, at : at + SUB, :] = imag

    count = samples.shape[2] // SUB
    parts = []
    for part in range(2):
        parts.append(
            jnp.concatenate(
                [samples[part, quad, pl.ds(baseline, count, stride=SUB), :] for quad in range(quads)], axis=1
            )
        )
    data = jnp.concatenate(parts, axis=0)
    high = data.astype(jnp.bfloat16)
    low = (data - high.astype(jnp.float32)).astype(jnp.bfloat16)
    mats = fringe_ref[...].reshape(2 * count, count)
    real, imag = mats[:count], mats[count:]
    both = jnp.concatenate(
        [jnp.concatenate([real, -imag], axis=1), jnp.concatenate([imag, real], axis=1)], axis=0
    )
    rated = jnp.dot(both, high, preferred_element_type=jnp.float32) + jnp.dot(
        both, low, preferred_element_type=jnp.float32
    )
    high = rated.astype(jnp.bfloat16)
    low = (rated - high.astype(jnp.float32)).astype(jnp.bfloat16)
    total = None
    wide = delay_ref.shape[3]
    for piece in range(delay_ref.shape[1]):
        for values in (high, low):
            term = lax.dot_general(
                values[:, piece * wide : (piece + 1) * wide],
                delay_ref[0, piece],
                (((1,), (1,)), ((), ())),
                preferred_element_type=jnp.float32,
            )
            total = term if total is None else total + term
    out_ref[...] = total.reshape(out_ref.shape)


def shards(visibility, groups, flags, fringe, delay):
    time_count = lax.axis_size("tm")
    chan_count = lax.axis_size("chan")
    everyone = ("tm", "chan")
    devices = time_count * chan_count
    total = groups.shape[0]
    own = total // devices
    times, chans = visibility.shape[2], visibility.shape[3]
    all_times, all_chans = times * time_count, chans * chan_count
    time_place = lax.axis_index("tm")
    chan_place = lax.axis_index("chan")
    place = jnp.stack([time_place, chan_place]).astype(jnp.int32)
    params = functools.partial(pltpu.CompilerParams, vmem_limit_bytes=VMEM)

    delay_groups = delay.shape[0]
    pieces = time_count // delay_groups
    wide = all_chans // pieces
    share = lax.dynamic_slice(
        delay, (time_place // pieces, 0, (time_place % pieces) * wide), (1, chans, wide)
    )
    share = lax.all_to_all(
        jnp.broadcast_to(share, (chan_count, chans, wide)), "chan", split_axis=0, concat_axis=0, tiled=True
    )
    delay_all = lax.all_gather(share.reshape(all_chans, wide), "tm", axis=0, tiled=True)
    delay_all = delay_all.reshape(delay_groups, pieces, all_chans, wide)

    rows = times * chans * SUB // LANES // SUB * own + 1
    step_lanes = 2 * LANES
    packed = pl.pallas_call(
        functools.partial(pack_kernel, rows=rows),
        grid=(total // step_lanes,),
        in_specs=[
            pl.BlockSpec((2, times, chans, step_lanes), lambda n: (0, 0, 0, n)),
            pl.BlockSpec((chans, step_lanes), lambda n: (0, n)),
        ],
        out_specs=pl.BlockSpec((step_lanes // SUB * rows, LANES), lambda n: (n, 0)),
        out_shape=jax.ShapeDtypeStruct((devices * rows, LANES), jnp.int32),
        compiler_params=params(),
        name="pack",
    )(jnp.transpose(visibility, (0, 2, 3, 1)), flags.T)
    words = lax.all_to_all(
        packed.reshape(devices, 1, rows * LANES), everyone, split_axis=0, concat_axis=0, tiled=True
    )
    words = words.reshape(time_count, chan_count * rows, LANES)

    held = fringe.shape[1]
    slab = 2 * all_times // time_count
    slabs = fringe.reshape(2, held, all_times // slab, slab, all_times)
    slabs = jnp.transpose(slabs, (0, 2, 1, 3, 4)).reshape(time_count, held, slab, all_times)
    table = lax.all_to_all(slabs, "tm", split_axis=0, concat_axis=0, tiled=True)
    table = table.reshape(time_count * held, slab, all_times)
    chosen = pl.pallas_call(
        select_kernel,
        grid_spec=pltpu.PrefetchScalarGridSpec(
            num_scalar_prefetch=2,
            grid=(),
            in_specs=[pl.BlockSpec(memory_space=pltpu.VMEM)],
            out_specs=pl.BlockSpec(memory_space=pltpu.VMEM),
        ),
        out_shape=jax.ShapeDtypeStruct((time_count, own, slab, all_times), jnp.bfloat16),
        compiler_params=params(),
        name="select",
    )(groups, place, table)
    mats = lax.all_to_all(chosen, "tm", split_axis=0, concat_axis=0, tiled=True)

    spread = time_count * held // delay_groups

    def delay_index(n, groups_ref, place_ref):
        mine = (place_ref[0] * chan_count + place_ref[1]) * own + n
        return (groups_ref[mine] // spread, 0, 0, 0)

    return pl.pallas_call(
        functools.partial(filter_kernel, rows=rows),
        grid_spec=pltpu.PrefetchScalarGridSpec(
            num_scalar_prefetch=2,
            grid=(own,),
            in_specs=[
                pl.BlockSpec((time_count, chan_count * rows, LANES), lambda n, *_: (0, 0, 0)),
                pl.BlockSpec((time_count, 1, slab, all_times), lambda n, *_: (0, n, 0, 0)),
                pl.BlockSpec((1, pieces, all_chans, wide), delay_index),
            ],
            out_specs=pl.BlockSpec((2, 1, all_times, all_chans), lambda n, *_: (0, n, 0, 0)),
            scratch_shapes=[
                pltpu.VMEM((LANES, devices), jnp.float32),
                pltpu.VMEM((2, all_chans // LANES, all_times * SUB, LANES), jnp.float32),
            ],
        ),
        out_shape=jax.ShapeDtypeStruct((2, own, all_times, all_chans), jnp.float32),
        compiler_params=params(),
        name="filter",
    )(groups, place, words, mats, delay_all)


def solution(mesh):
    placed = (
        P(None, None, "tm", "chan"),
        P(),
        P(None, "chan"),
        P(None, "tm", None, None),
        P(None, "chan", None),
    )
    return jax.shard_map(
        shards,
        mesh=mesh,
        in_specs=placed,
        out_specs=P(None, ("tm", "chan"), None, None),
        check_vma=False,
    )
```

```python
import functools

import jax
import jax.numpy as jnp
from jax import lax
from jax.experimental import pallas as pl
from jax.experimental.pallas import tpu as pltpu
from jax.sharding import PartitionSpec as P

LANES = 128
SUB = 8
FULL = 32760.0
MIDDLE = 32768.0
VMEM = 56 * 1024 * 1024
CORES = 2


def pack_kernel(vis_ref, flag_ref, out_ref, rows):
    for tile in range(vis_ref.shape[3] // LANES):
        lanes = pl.ds(tile * LANES, LANES)
        keep = flag_ref[:, lanes].astype(jnp.float32)
        masked = vis_ref[:, :, :, lanes] * keep[None, None]
        loudest = jnp.max(jnp.abs(masked), axis=(0, 1, 2), keepdims=True)
        level = jnp.ceil(jnp.log2(jnp.maximum(loudest, 1e-30)) * 4.0)
        factor = FULL / jnp.exp2(level * 0.25)
        coded = (masked * factor + (MIDDLE + 0.5)).astype(jnp.int32)
        words = coded[0] | (coded[1] << 16)
        level_row = level.reshape(1, LANES).astype(jnp.int32)
        times, chans = words.shape[0], words.shape[1]
        fold = LANES // chans
        for part in range(times // fold):
            turned = words[part * fold : (part + 1) * fold].reshape(LANES, LANES).T
            for owner in range(LANES // SUB):
                place = (tile * (LANES // SUB) + owner) * rows + part * SUB
                out_ref[place : place + SUB, :] = turned[owner * SUB : (owner + 1) * SUB]
        for owner in range(LANES // SUB):
            place = (tile * (LANES // SUB) + owner) * rows + rows - 1
            out_ref[place : place + 1, :] = level_row


def shares_kernel(place_ref, fringe_ref, *out_refs):
    halves, pieces = fringe_ref.shape[0], fringe_ref.shape[2]
    for core, out_ref in enumerate(out_refs):
        for chip in range(out_ref.shape[0]):
            slab = place_ref[0] ^ (chip * CORES + core)
            out_ref[chip] = fringe_ref[slab // pieces, :, lax.rem(slab, pieces)]


def regroup_kernel(*refs):
    for core in range(CORES):
        for chip, out_ref in enumerate(refs[CORES:]):
            out_ref[core] = refs[core][chip]


def select_kernel(groups_ref, place_ref, *refs):
    in_refs, out_refs, table = refs[: -CORES - 1], refs[-CORES - 1 : -1], refs[-1]
    count, held, each = table.shape[0], table.shape[1], out_refs[0].shape[1]
    chan_count = groups_ref.shape[0] // (count * each)
    for chip, in_ref in enumerate(in_refs):
        for core in range(CORES):
            table[place_ref[0] ^ (chip * CORES + core)] = in_ref[core]
    for core, out_ref in enumerate(out_refs):
        for chip in range(out_ref.shape[0]):
            owner = place_ref[0] ^ (chip * CORES + core)
            for slot in range(each):
                group = groups_ref[(owner * chan_count + place_ref[1]) * each + slot]
                out_ref[chip, slot] = table[group // held, lax.rem(group, held)]


def filter_kernel(groups_ref, place_ref, words_ref, delay_ref, *refs, rows, spread):
    fringe_refs = refs[:-10]
    out_ref, words, levels, samples, slabs, mats, delay, word_sems, slab_sems, delay_sems = refs[-10:]
    baseline = pl.program_id(0)
    baselines = pl.num_programs(0)
    blocks = words_ref.shape[0]
    chan_count = words_ref.shape[1] // rows
    quads = chan_count // 4
    slot = lax.rem(baseline, 2)

    def fetch_words(block):
        return pltpu.make_async_copy(words_ref.at[block], words.at[block], word_sems.at[block])

    def fetch_slabs(chip):
        return pltpu.make_async_copy(fringe_refs[chip], slabs.at[chip], slab_sems.at[chip])

    def fetch_delay(number, to):
        mine = (place_ref[0] * chan_count + place_ref[1]) * baselines + number
        group = groups_ref[mine] // spread
        return pltpu.make_async_copy(delay_ref.at[group], delay.at[to], delay_sems.at[to])

    @pl.when(baseline == 0)
    def unpack():
        for block in range(blocks):
            fetch_words(block).start()
        for chip in range(len(fringe_refs)):
            fetch_slabs(chip).start()
        fetch_delay(0, 0).start()
        lane = lax.broadcasted_iota(jnp.int32, (SUB, LANES), 1)
        low_half = lane < 64
        even_group = (lane & 32) == 0
        group = lane // 32
        for block in range(blocks):
            fetch_words(block).wait()
            level = words[block, pl.ds(rows - 1, chan_count, stride=rows), :].astype(jnp.float32)
            scales = jnp.exp2(level * 0.25) * (1.0 / FULL)
            scales = jnp.concatenate([scales, jnp.zeros((LANES - chan_count, LANES), jnp.float32)], axis=0)
            levels[...] = scales.T
            own = levels[pl.ds(pl.multiple_of(place_ref[1] * SUB, SUB), SUB), :]
            for quad in range(quads):
                first = quad * 4
                scale = jnp.broadcast_to(own[:, first : first + 1], (SUB, LANES))
                for member in range(1, 4):
                    other = jnp.broadcast_to(own[:, first + member : first + member + 1], (SUB, LANES))
                    scale = jnp.where(group == member, other, scale)
                offset = scale * -MIDDLE
                for half in range((rows - 1) // SUB):
                    v = [
                        words[block, pl.ds((quad * 4 + member) * rows + half * SUB, SUB), :]
                        for member in range(4)
                    ]
                    r = [pltpu.roll(x, 64, 1) for x in v]
                    a0 = jnp.where(low_half, v[0], r[2])
                    a2 = jnp.where(low_half, r[0], v[2])
                    a1 = jnp.where(low_half, v[1], r[3])
                    a3 = jnp.where(low_half, r[1], v[3])
                    turned = (
                        jnp.where(even_group, a0, pltpu.roll(a1, 32, 1)),
                        jnp.where(even_group, pltpu.roll(a0, 96, 1), a1),
                        jnp.where(even_group, a2, pltpu.roll(a3, 32, 1)),
                        jnp.where(even_group, pltpu.roll(a2, 96, 1), a3),
                    )
                    for step, word in enumerate(turned):
                        at = (block * 8 + half * 4 + step) * SUB
                        real = (word & 0xFFFF).astype(jnp.float32) * scale + offset
                        imag = lax.shift_right_logical(word, 16).astype(jnp.float32) * scale + offset
                        samples[0, quad, at : at + SUB, :] = real
                        samples[1, quad, at : at + SUB, :] = imag
        for chip in range(len(fringe_refs)):
            fetch_slabs(chip).wait()

    @pl.when(baseline + 1 < baselines)
    def ahead():
        fetch_delay(baseline + 1, 1 - slot).start()

    count = samples.shape[2] // SUB
    parts = []
    for part in range(2):
        parts.append(
            jnp.concatenate(
                [samples[part, quad, pl.ds(baseline, count, stride=SUB), :] for quad in range(quads)], axis=1
            )
        )
    data = jnp.concatenate(parts, axis=0)
    high = data.astype(jnp.bfloat16)
    low = (data - high.astype(jnp.float32)).astype(jnp.bfloat16)
    for chip in range(len(fringe_refs)):
        for core in range(CORES):
            mats[place_ref[0] ^ (chip * CORES + core)] = slabs[chip, core, baseline]
    whole = mats[...].reshape(2 * count, count)
    real, imag = whole[:count], whole[count:]
    both = jnp.concatenate(
        [jnp.concatenate([real, -imag], axis=1), jnp.concatenate([imag, real], axis=1)], axis=0
    )
    rated = jnp.dot(both, high, preferred_element_type=jnp.float32) + jnp.dot(
        both, low, preferred_element_type=jnp.float32
    )
    high = rated.astype(jnp.bfloat16)
    low = (rated - high.astype(jnp.float32)).astype(jnp.bfloat16)
    fetch_delay(baseline, slot).wait()
    both = jnp.concatenate([high, low], axis=0)
    wide = delay.shape[3]
    total = None
    for piece in range(delay.shape[1]):
        term = lax.dot_general(
            both[:, piece * wide : (piece + 1) * wide],
            delay[slot, piece],
            (((1,), (1,)), ((), ())),
            preferred_element_type=jnp.float32,
        )
        total = term if total is None else total + term
    out_ref[...] = (total[: 2 * count] + total[2 * count :]).reshape(out_ref.shape)


def shards(visibility, groups, flags, fringe, delay):
    time_count = lax.axis_size("tm")
    chan_count = lax.axis_size("chan")
    everyone = ("tm", "chan")
    devices = time_count * chan_count
    total = groups.shape[0]
    own = total // devices
    times, chans = visibility.shape[2], visibility.shape[3]
    all_times, all_chans = times * time_count, chans * chan_count
    time_place = lax.axis_index("tm")
    chan_place = lax.axis_index("chan")
    place = jnp.stack([time_place, chan_place]).astype(jnp.int32)
    params = functools.partial(pltpu.CompilerParams, vmem_limit_bytes=VMEM)

    delay_groups = delay.shape[0]
    pieces = time_count // delay_groups
    wide = all_chans // pieces
    share = lax.dynamic_slice(
        delay, (time_place // pieces, 0, (time_place % pieces) * wide), (1, chans, wide)
    )
    share = lax.all_to_all(
        jnp.broadcast_to(share, (chan_count, chans, wide)), "chan", split_axis=0, concat_axis=0, tiled=True
    )

    rows = times * chans * SUB // LANES // SUB * own + 1
    step_lanes = 2 * LANES
    packed = pl.pallas_call(
        functools.partial(pack_kernel, rows=rows),
        grid=(total // step_lanes,),
        in_specs=[
            pl.BlockSpec((2, times, chans, step_lanes), lambda n: (0, 0, 0, n)),
            pl.BlockSpec((chans, step_lanes), lambda n: (0, n)),
        ],
        out_specs=pl.BlockSpec((step_lanes // SUB * rows, LANES), lambda n: (n, 0)),
        out_shape=jax.ShapeDtypeStruct((devices * rows, LANES), jnp.int32),
        compiler_params=params(),
        name="pack",
    )(jnp.transpose(visibility, (0, 2, 3, 1)), flags.T)
    share, fringe, packed = lax.optimization_barrier((share, fringe, packed))
    delay_all = lax.all_gather(share.reshape(all_chans, wide), "tm", axis=0, tiled=True)
    delay_all = delay_all.reshape(delay_groups, pieces, all_chans, wide)
    words = lax.all_to_all(
        packed.reshape(devices, 1, rows * LANES), everyone, split_axis=0, concat_axis=0, tiled=True
    )
    words = words.reshape(time_count, chan_count * rows, LANES)

    def crossed(array, mask):
        return lax.ppermute(array, "tm", [(k, k ^ mask) for k in range(time_count)]) if mask else array

    chips = time_count // CORES
    held = fringe.shape[1]
    slab = 2 * all_times // time_count
    inside = pl.BlockSpec(memory_space=pltpu.VMEM)

    def exchanged(arrays):
        _, *block = arrays[0].shape
        turned = pl.pallas_call(
            regroup_kernel,
            in_specs=[inside] * CORES,
            out_specs=[inside] * chips,
            out_shape=[jax.ShapeDtypeStruct((CORES, *block), jnp.bfloat16)] * chips,
            compiler_params=params(),
            name="regroup",
        )(*[crossed(array, core) for core, array in enumerate(arrays)])
        return [crossed(array, chip * CORES) for chip, array in enumerate(turned)]

    shares = pl.pallas_call(
        shares_kernel,
        grid_spec=pltpu.PrefetchScalarGridSpec(
            num_scalar_prefetch=1, grid=(), in_specs=[inside], out_specs=[inside] * CORES
        ),
        out_shape=[jax.ShapeDtypeStruct((chips, held, slab, all_times), jnp.bfloat16)] * CORES,
        compiler_params=params(),
        name="shares",
    )(place, fringe.reshape(2, held, all_times // slab, slab, all_times))
    chosen = pl.pallas_call(
        select_kernel,
        grid_spec=pltpu.PrefetchScalarGridSpec(
            num_scalar_prefetch=2,
            grid=(),
            in_specs=[inside] * chips,
            out_specs=[inside] * CORES,
            scratch_shapes=[pltpu.VMEM((time_count, held, slab, all_times), jnp.bfloat16)],
        ),
        out_shape=[jax.ShapeDtypeStruct((chips, own, slab, all_times), jnp.bfloat16)] * CORES,
        compiler_params=params(),
        name="select",
    )(groups, place, *exchanged(shares))
    mats = exchanged(chosen)

    spread = time_count * held // delay_groups

    return pl.pallas_call(
        functools.partial(filter_kernel, rows=rows, spread=spread),
        grid_spec=pltpu.PrefetchScalarGridSpec(
            num_scalar_prefetch=2,
            grid=(own,),
            in_specs=[pl.BlockSpec(memory_space=pl.ANY)] * (2 + chips),
            out_specs=pl.BlockSpec((2, 1, all_times, all_chans), lambda n, *_: (0, n, 0, 0)),
            scratch_shapes=[
                pltpu.VMEM((time_count, chan_count * rows, LANES), jnp.int32),
                pltpu.VMEM((LANES, LANES), jnp.float32),
                pltpu.VMEM((2, all_chans // LANES, all_times * SUB, LANES), jnp.float32),
                pltpu.VMEM((chips, CORES, own, slab, all_times), jnp.bfloat16),
                pltpu.VMEM((time_count, slab, all_times), jnp.bfloat16),
                pltpu.VMEM((2, pieces, all_chans, wide), jnp.bfloat16),
                pltpu.SemaphoreType.DMA((time_count,)),
                pltpu.SemaphoreType.DMA((chips,)),
                pltpu.SemaphoreType.DMA((2,)),
            ],
        ),
        out_shape=jax.ShapeDtypeStruct((2, own, all_times, all_chans), jnp.float32),
        compiler_params=params(),
        name="filter",
    )(groups, place, words, delay_all, *mats)


def solution(mesh):
    placed = (
        P(None, None, "tm", "chan"),
        P(),
        P(None, "chan"),
        P(None, "tm", None, None),
        P(None, "chan", None),
    )
    return jax.shard_map(
        shards,
        mesh=mesh,
        in_specs=placed,
        out_specs=P(None, ("tm", "chan"), None, None),
        check_vma=False,
    )
```

```python
import functools

import jax
import jax.numpy as jnp
from jax import lax
from jax.experimental import pallas as pl
from jax.experimental.pallas import tpu as pltpu
from jax.sharding import PartitionSpec as P

LANES = 128
SUB = 8
FULL = 32760.0
MIDDLE = 32768.0
VMEM = 32 * 1024 * 1024
FILTER_VMEM = 60 * 1024 * 1024
CORES = 2


def pack_kernel(vis_ref, flag_ref, out_ref, rows):
    for tile in range(vis_ref.shape[3] // LANES):
        lanes = pl.ds(tile * LANES, LANES)
        keep = flag_ref[:, lanes].astype(jnp.float32)
        masked = vis_ref[:, :, :, lanes] * keep[None, None]
        loudest = jnp.max(jnp.abs(masked), axis=(0, 1, 2), keepdims=True)
        level = jnp.ceil(jnp.log2(jnp.maximum(loudest, 1e-30)) * 4.0)
        factor = FULL / jnp.exp2(level * 0.25)
        coded = (masked * factor + (MIDDLE + 0.5)).astype(jnp.int32)
        words = coded[0] | (coded[1] << 16)
        level_row = level.reshape(1, LANES).astype(jnp.int32)
        times, chans = words.shape[0], words.shape[1]
        fold = LANES // chans
        for part in range(times // fold):
            turned = words[part * fold : (part + 1) * fold].reshape(LANES, LANES).T
            for owner in range(LANES // SUB):
                place = (tile * (LANES // SUB) + owner) * rows + part * SUB
                out_ref[place : place + SUB, :] = turned[owner * SUB : (owner + 1) * SUB]
        for owner in range(LANES // SUB):
            place = (tile * (LANES // SUB) + owner) * rows + rows - 1
            out_ref[place : place + 1, :] = level_row


def shares_kernel(place_ref, fringe_ref, *out_refs):
    halves, pieces = fringe_ref.shape[0], fringe_ref.shape[2]
    for core, out_ref in enumerate(out_refs):
        for chip in range(out_ref.shape[0]):
            slab = place_ref[0] ^ (chip * CORES + core)
            out_ref[chip] = fringe_ref[slab // pieces, :, lax.rem(slab, pieces)]


def regroup_kernel(*refs):
    for core in range(CORES):
        for chip, out_ref in enumerate(refs[CORES:]):
            out_ref[core] = refs[core][chip]


def select_kernel(groups_ref, place_ref, *refs):
    in_refs, out_refs, table = refs[: -CORES - 1], refs[-CORES - 1 : -1], refs[-1]
    count, held, each = table.shape[0], table.shape[1], out_refs[0].shape[1]
    chan_count = groups_ref.shape[0] // (count * each)
    for chip, in_ref in enumerate(in_refs):
        for core in range(CORES):
            table[place_ref[0] ^ (chip * CORES + core)] = in_ref[core]
    for core, out_ref in enumerate(out_refs):
        for chip in range(out_ref.shape[0]):
            owner = place_ref[0] ^ (chip * CORES + core)
            for slot in range(each):
                group = groups_ref[(owner * chan_count + place_ref[1]) * each + slot]
                out_ref[chip, slot] = table[group // held, lax.rem(group, held)]


def filter_kernel(groups_ref, place_ref, words_ref, delay_ref, *refs, rows, spread):
    fringe_refs = refs[:-12]
    out_ref, words, levels, samples, slabs, mats, delay, results, *sems = refs[-12:]
    word_sems, slab_sems, delay_sems, out_sems = sems
    baselines = delay.shape[0]
    blocks = words_ref.shape[0]
    chan_count = words_ref.shape[1] // rows
    quads = chan_count // 4

    def fetch_words(block):
        return pltpu.make_async_copy(words_ref.at[block], words.at[block], word_sems.at[block])

    def fetch_slabs(chip):
        return pltpu.make_async_copy(fringe_refs[chip], slabs.at[chip], slab_sems.at[chip])

    def fetch_delay(baseline, piece):
        mine = (place_ref[0] * chan_count + place_ref[1]) * baselines + baseline
        group = groups_ref[mine] // spread
        return pltpu.make_async_copy(
            delay_ref.at[group, piece], delay.at[baseline, piece], delay_sems.at[baseline, piece]
        )

    def send_out(baseline, slot, part):
        return pltpu.make_async_copy(
            results.at[slot, part], out_ref.at[part, baseline], out_sems.at[slot, part]
        )

    def unpack():
        for block in range(blocks):
            fetch_words(block).start()
        for chip in range(len(fringe_refs)):
            fetch_slabs(chip).start()
        lane = lax.broadcasted_iota(jnp.int32, (SUB, LANES), 1)
        low_half = lane < 64
        even_group = (lane & 32) == 0
        group = lane // 32
        def unpack_block(block, carry):
            fetch_words(block).wait()
            fetch_delay(block // delay.shape[1], lax.rem(block, delay.shape[1])).start()
            level = words[block, pl.ds(rows - 1, chan_count, stride=rows), :].astype(jnp.float32)
            scales = jnp.exp2(level * 0.25) * (1.0 / FULL)
            scales = jnp.concatenate([scales, jnp.zeros((LANES - chan_count, LANES), jnp.float32)], axis=0)
            levels[...] = scales.T
            own = levels[pl.ds(pl.multiple_of(place_ref[1] * SUB, SUB), SUB), :]
            for quad in range(quads):
                first = quad * 4
                scale = jnp.broadcast_to(own[:, first : first + 1], (SUB, LANES))
                for member in range(1, 4):
                    other = jnp.broadcast_to(own[:, first + member : first + member + 1], (SUB, LANES))
                    scale = jnp.where(group == member, other, scale)
                offset = scale * -MIDDLE
                for half in range((rows - 1) // SUB):
                    v = [
                        words[block, pl.ds((quad * 4 + member) * rows + half * SUB, SUB), :]
                        for member in range(4)
                    ]
                    r = [pltpu.roll(x, 64, 1) for x in v]
                    a0 = jnp.where(low_half, v[0], r[2])
                    a2 = jnp.where(low_half, r[0], v[2])
                    a1 = jnp.where(low_half, v[1], r[3])
                    a3 = jnp.where(low_half, r[1], v[3])
                    turned = (
                        jnp.where(even_group, a0, pltpu.roll(a1, 32, 1)),
                        jnp.where(even_group, pltpu.roll(a0, 96, 1), a1),
                        jnp.where(even_group, a2, pltpu.roll(a3, 32, 1)),
                        jnp.where(even_group, pltpu.roll(a2, 96, 1), a3),
                    )
                    for step, word in enumerate(turned):
                        at = pl.ds(pl.multiple_of((block * 8 + half * 4 + step) * SUB, SUB), SUB)
                        real = (word & 0xFFFF).astype(jnp.float32) * scale + offset
                        imag = lax.shift_right_logical(word, 16).astype(jnp.float32) * scale + offset
                        samples[0, quad, at, :] = real
                        samples[1, quad, at, :] = imag
            return carry

        lax.fori_loop(0, blocks, unpack_block, 0)
        for chip in range(len(fringe_refs)):
            fetch_slabs(chip).wait()

    unpack()
    count = samples.shape[2] // SUB

    def over_time(baseline):
        parts = []
        for part in range(2):
            parts.append(
                jnp.concatenate(
                    [samples[part, quad, pl.ds(baseline, count, stride=SUB), :] for quad in range(quads)], axis=1
                )
            )
        data = jnp.concatenate(parts, axis=0)
        high = data.astype(jnp.bfloat16)
        low = (data - high.astype(jnp.float32)).astype(jnp.bfloat16)
        for chip in range(len(fringe_refs)):
            for core in range(CORES):
                mats[place_ref[0] ^ (chip * CORES + core)] = slabs[chip, core, baseline]
        whole = mats[...].reshape(2 * count, count)
        real, imag = whole[:count], whole[count:]
        both = jnp.concatenate(
            [jnp.concatenate([real, -imag], axis=1), jnp.concatenate([imag, real], axis=1)], axis=0
        )
        rated = jnp.dot(both, high, preferred_element_type=jnp.float32) + jnp.dot(
            both, low, preferred_element_type=jnp.float32
        )
        high = rated.astype(jnp.bfloat16)
        low = (rated - high.astype(jnp.float32)).astype(jnp.bfloat16)
        return jnp.concatenate([high, low], axis=0)

    def over_channels(baseline, both):
        slot = baseline % results.shape[0]
        wide = delay.shape[3]
        for piece in range(delay.shape[1]):
            fetch_delay(baseline, piece).wait()
        if baseline >= results.shape[0]:
            for part in range(2):
                send_out(baseline, slot, part).wait()
        for part in range(2):
            rowsel = jnp.concatenate(
                [both[part * count : (part + 1) * count], both[(2 + part) * count : (3 + part) * count]], axis=0
            )
            total = None
            for piece in range(delay.shape[1]):
                term = lax.dot_general(
                    rowsel[:, piece * wide : (piece + 1) * wide],
                    delay[baseline, piece],
                    (((1,), (1,)), ((), ())),
                    preferred_element_type=jnp.float32,
                )
                total = term if total is None else total + term
            results[slot, part] = total[:count] + total[count:]
            send_out(baseline, slot, part).start()

    ready = over_time(0)
    for baseline in range(baselines):
        following = over_time(baseline + 1) if baseline + 1 < baselines else None
        over_channels(baseline, ready)
        ready = following
    for baseline in range(baselines - results.shape[0], baselines):
        for part in range(2):
            send_out(baseline, baseline % results.shape[0], part).wait()


def shards(visibility, groups, flags, fringe, delay):
    time_count = lax.axis_size("tm")
    chan_count = lax.axis_size("chan")
    everyone = ("tm", "chan")
    devices = time_count * chan_count
    total = groups.shape[0]
    own = total // devices
    times, chans = visibility.shape[2], visibility.shape[3]
    all_times, all_chans = times * time_count, chans * chan_count
    time_place = lax.axis_index("tm")
    chan_place = lax.axis_index("chan")
    place = jnp.stack([time_place, chan_place]).astype(jnp.int32)
    params = functools.partial(pltpu.CompilerParams, vmem_limit_bytes=VMEM)

    delay_groups = delay.shape[0]
    pieces = time_count // delay_groups
    wide = all_chans // pieces
    share = lax.dynamic_slice(
        delay, (time_place // pieces, 0, (time_place % pieces) * wide), (1, chans, wide)
    )
    share = lax.all_to_all(
        jnp.broadcast_to(share, (chan_count, chans, wide)), "chan", split_axis=0, concat_axis=0, tiled=True
    )

    rows = times * chans * SUB // LANES // SUB * own + 1
    step_lanes = 2 * LANES
    packed = pl.pallas_call(
        functools.partial(pack_kernel, rows=rows),
        grid=(total // step_lanes,),
        in_specs=[
            pl.BlockSpec((2, times, chans, step_lanes), lambda n: (0, 0, 0, n)),
            pl.BlockSpec((chans, step_lanes), lambda n: (0, n)),
        ],
        out_specs=pl.BlockSpec((step_lanes // SUB * rows, LANES), lambda n: (n, 0)),
        out_shape=jax.ShapeDtypeStruct((devices * rows, LANES), jnp.int32),
        compiler_params=params(),
        name="pack",
    )(jnp.transpose(visibility, (0, 2, 3, 1)), flags.T)
    share, fringe, packed = lax.optimization_barrier((share, fringe, packed))
    delay_all = lax.all_gather(share.reshape(all_chans, wide), "tm", axis=0, tiled=True)
    delay_all = delay_all.reshape(delay_groups, pieces, all_chans, wide)
    words = lax.all_to_all(
        packed.reshape(devices, 1, rows * LANES), everyone, split_axis=0, concat_axis=0, tiled=True
    )
    words = words.reshape(time_count, chan_count * rows, LANES)

    def crossed(array, mask):
        return lax.ppermute(array, "tm", [(k, k ^ mask) for k in range(time_count)]) if mask else array

    chips = time_count // CORES
    held = fringe.shape[1]
    slab = 2 * all_times // time_count
    inside = pl.BlockSpec(memory_space=pltpu.VMEM)

    def exchanged(arrays):
        _, *block = arrays[0].shape
        turned = pl.pallas_call(
            regroup_kernel,
            in_specs=[inside] * CORES,
            out_specs=[inside] * chips,
            out_shape=[jax.ShapeDtypeStruct((CORES, *block), jnp.bfloat16)] * chips,
            compiler_params=params(),
            name="regroup",
        )(*[crossed(array, core) for core, array in enumerate(arrays)])
        return [crossed(array, chip * CORES) for chip, array in enumerate(turned)]

    shares = pl.pallas_call(
        shares_kernel,
        grid_spec=pltpu.PrefetchScalarGridSpec(
            num_scalar_prefetch=1, grid=(), in_specs=[inside], out_specs=[inside] * CORES
        ),
        out_shape=[jax.ShapeDtypeStruct((chips, held, slab, all_times), jnp.bfloat16)] * CORES,
        compiler_params=params(),
        name="shares",
    )(place, fringe.reshape(2, held, all_times // slab, slab, all_times))
    chosen = pl.pallas_call(
        select_kernel,
        grid_spec=pltpu.PrefetchScalarGridSpec(
            num_scalar_prefetch=2,
            grid=(),
            in_specs=[inside] * chips,
            out_specs=[inside] * CORES,
            scratch_shapes=[pltpu.VMEM((time_count, held, slab, all_times), jnp.bfloat16)],
        ),
        out_shape=[jax.ShapeDtypeStruct((chips, own, slab, all_times), jnp.bfloat16)] * CORES,
        compiler_params=params(),
        name="select",
    )(groups, place, *exchanged(shares))
    mats = exchanged(chosen)

    spread = time_count * held // delay_groups

    return pl.pallas_call(
        functools.partial(filter_kernel, rows=rows, spread=spread),
        grid_spec=pltpu.PrefetchScalarGridSpec(
            num_scalar_prefetch=2,
            grid=(),
            in_specs=[pl.BlockSpec(memory_space=pltpu.HBM)] * 2 + [pl.BlockSpec(memory_space=pl.ANY)] * chips,
            out_specs=pl.BlockSpec(memory_space=pl.ANY),
            scratch_shapes=[
                pltpu.VMEM((time_count, chan_count * rows, LANES), jnp.int32),
                pltpu.VMEM((LANES, LANES), jnp.float32),
                pltpu.VMEM((2, all_chans // LANES, all_times * SUB, LANES), jnp.float32),
                pltpu.VMEM((chips, CORES, own, slab, all_times), jnp.bfloat16),
                pltpu.VMEM((time_count, slab, all_times), jnp.bfloat16),
                pltpu.VMEM((own, pieces, all_chans, wide), jnp.bfloat16),
                pltpu.VMEM((4, 2, all_times, all_chans), jnp.float32),
                pltpu.SemaphoreType.DMA((time_count,)),
                pltpu.SemaphoreType.DMA((chips,)),
                pltpu.SemaphoreType.DMA((own, pieces)),
                pltpu.SemaphoreType.DMA((4, 2)),
            ],
        ),
        out_shape=jax.ShapeDtypeStruct((2, own, all_times, all_chans), jnp.float32),
        compiler_params=pltpu.CompilerParams(vmem_limit_bytes=FILTER_VMEM),
        name="filter",
    )(groups, place, words, delay_all, *mats)


def solution(mesh):
    placed = (
        P(None, None, "tm", "chan"),
        P(),
        P(None, "chan"),
        P(None, "tm", None, None),
        P(None, "chan", None),
    )
    return jax.shard_map(
        shards,
        mesh=mesh,
        in_specs=placed,
        out_specs=P(None, ("tm", "chan"), None, None),
        check_vma=False,
    )
```

```python
import functools

import jax
import jax.numpy as jnp
from jax import lax
from jax.experimental import pallas as pl
from jax.experimental.pallas import tpu as pltpu
from jax.sharding import PartitionSpec as P

LANES = 128
SUB = 8
FULL = 32760.0
MIDDLE = 32768.0
VMEM = 32 * 1024 * 1024
LARGE_VMEM = 60 * 1024 * 1024
CORES = 2


def pack_kernel(vis_ref, flag_ref, out_ref, vis, flag, packed, vis_sems, flag_sem, out_sems, *, rows):
    steps, lanes = vis.shape[0], vis.shape[4]
    owners = LANES // SUB

    def fetch_vis(step):
        there = pl.ds(pl.multiple_of(step * lanes, lanes), lanes)
        return pltpu.make_async_copy(vis_ref.at[:, :, :, there], vis.at[step], vis_sems.at[step])

    def fetch_flag():
        return pltpu.make_async_copy(flag_ref, flag, flag_sem)

    def send_out(step):
        there = pl.ds(pl.multiple_of(step * packed.shape[1], SUB), packed.shape[1])
        return pltpu.make_async_copy(packed.at[step], out_ref.at[there], out_sems.at[step])

    fetch_flag().start()
    for step in range(steps):
        fetch_vis(step).start()
    fetch_flag().wait()

    def one(step, carry):
        fetch_vis(step).wait()
        for tile in range(lanes // LANES):
            here = pl.ds(tile * LANES, LANES)
            keep = flag[:, pl.ds(pl.multiple_of(step * lanes + tile * LANES, LANES), LANES)].astype(jnp.float32)
            masked = vis[step, :, :, :, here] * keep[None, None]
            loudest = jnp.max(jnp.abs(masked), axis=(0, 1, 2), keepdims=True)
            level = jnp.ceil(jnp.log2(jnp.maximum(loudest, 1e-30)) * 4.0)
            factor = FULL / jnp.exp2(level * 0.25)
            coded = (masked * factor + (MIDDLE + 0.5)).astype(jnp.int32)
            words = coded[0] | (coded[1] << 16)
            level_row = level.reshape(1, LANES).astype(jnp.int32)
            times, chans = words.shape[0], words.shape[1]
            fold = LANES // chans
            for part in range(times // fold):
                turned = words[part * fold : (part + 1) * fold].reshape(LANES, LANES).T
                for owner in range(owners):
                    place = (tile * owners + owner) * rows + part * SUB
                    packed[step, place : place + SUB, :] = turned[owner * SUB : (owner + 1) * SUB]
            for owner in range(owners):
                place = (tile * owners + owner) * rows + rows - 1
                packed[step, place : place + 1, :] = level_row
        send_out(step).start()
        return carry

    lax.fori_loop(0, steps, one, 0)
    for step in range(steps):
        send_out(step).wait()


def shares_kernel(place_ref, fringe_ref, *out_refs):
    halves, pieces = fringe_ref.shape[0], fringe_ref.shape[2]
    for core, out_ref in enumerate(out_refs):
        for chip in range(out_ref.shape[0]):
            slab = place_ref[0] ^ (chip * CORES + core)
            out_ref[chip] = fringe_ref[slab // pieces, :, lax.rem(slab, pieces)]


def regroup_kernel(*refs):
    for core in range(CORES):
        for chip, out_ref in enumerate(refs[CORES:]):
            out_ref[core] = refs[core][chip]


def select_kernel(groups_ref, place_ref, *refs):
    in_refs, out_refs, table = refs[: -CORES - 1], refs[-CORES - 1 : -1], refs[-1]
    count, held, each = table.shape[0], table.shape[1], out_refs[0].shape[1]
    chan_count = groups_ref.shape[0] // (count * each)
    for chip, in_ref in enumerate(in_refs):
        for core in range(CORES):
            table[place_ref[0] ^ (chip * CORES + core)] = in_ref[core]
    for core, out_ref in enumerate(out_refs):
        for chip in range(out_ref.shape[0]):
            owner = place_ref[0] ^ (chip * CORES + core)
            for slot in range(each):
                group = groups_ref[(owner * chan_count + place_ref[1]) * each + slot]
                out_ref[chip, slot] = table[group // held, lax.rem(group, held)]


def filter_kernel(groups_ref, place_ref, words_ref, delay_ref, *refs, rows, spread):
    fringe_refs = refs[:-12]
    out_ref, words, levels, samples, slabs, mats, delay, results, *sems = refs[-12:]
    word_sems, slab_sems, delay_sems, out_sems = sems
    baselines = delay.shape[0]
    blocks = words_ref.shape[0]
    chan_count = words_ref.shape[1] // rows
    quads = chan_count // 4

    def fetch_words(block):
        return pltpu.make_async_copy(words_ref.at[block], words.at[block], word_sems.at[block])

    def fetch_slabs(chip):
        return pltpu.make_async_copy(fringe_refs[chip], slabs.at[chip], slab_sems.at[chip])

    def fetch_delay(baseline, piece):
        mine = (place_ref[0] * chan_count + place_ref[1]) * baselines + baseline
        group = groups_ref[mine] // spread
        return pltpu.make_async_copy(
            delay_ref.at[group, piece], delay.at[baseline, piece], delay_sems.at[baseline, piece]
        )

    def send_out(baseline, slot, part):
        return pltpu.make_async_copy(
            results.at[slot, part], out_ref.at[part, baseline], out_sems.at[slot, part]
        )

    def unpack():
        for block in range(blocks):
            fetch_words(block).start()
        for chip in range(len(fringe_refs)):
            fetch_slabs(chip).start()
        lane = lax.broadcasted_iota(jnp.int32, (SUB, LANES), 1)
        low_half = lane < 64
        even_group = (lane & 32) == 0
        group = lane // 32
        def unpack_block(block, carry):
            fetch_words(block).wait()
            fetch_delay(block // delay.shape[1], lax.rem(block, delay.shape[1])).start()
            level = words[block, pl.ds(rows - 1, chan_count, stride=rows), :].astype(jnp.float32)
            scales = jnp.exp2(level * 0.25) * (1.0 / FULL)
            scales = jnp.concatenate([scales, jnp.zeros((LANES - chan_count, LANES), jnp.float32)], axis=0)
            levels[...] = scales.T
            own = levels[pl.ds(pl.multiple_of(place_ref[1] * SUB, SUB), SUB), :]
            for quad in range(quads):
                first = quad * 4
                scale = jnp.broadcast_to(own[:, first : first + 1], (SUB, LANES))
                for member in range(1, 4):
                    other = jnp.broadcast_to(own[:, first + member : first + member + 1], (SUB, LANES))
                    scale = jnp.where(group == member, other, scale)
                offset = scale * -MIDDLE
                for half in range((rows - 1) // SUB):
                    v = [
                        words[block, pl.ds((quad * 4 + member) * rows + half * SUB, SUB), :]
                        for member in range(4)
                    ]
                    r = [pltpu.roll(x, 64, 1) for x in v]
                    a0 = jnp.where(low_half, v[0], r[2])
                    a2 = jnp.where(low_half, r[0], v[2])
                    a1 = jnp.where(low_half, v[1], r[3])
                    a3 = jnp.where(low_half, r[1], v[3])
                    turned = (
                        jnp.where(even_group, a0, pltpu.roll(a1, 32, 1)),
                        jnp.where(even_group, pltpu.roll(a0, 96, 1), a1),
                        jnp.where(even_group, a2, pltpu.roll(a3, 32, 1)),
                        jnp.where(even_group, pltpu.roll(a2, 96, 1), a3),
                    )
                    for step, word in enumerate(turned):
                        at = pl.ds(pl.multiple_of((block * 8 + half * 4 + step) * SUB, SUB), SUB)
                        real = (word & 0xFFFF).astype(jnp.float32) * scale + offset
                        imag = lax.shift_right_logical(word, 16).astype(jnp.float32) * scale + offset
                        samples[0, quad, at, :] = real
                        samples[1, quad, at, :] = imag
            return carry

        lax.fori_loop(0, blocks, unpack_block, 0)
        for chip in range(len(fringe_refs)):
            fetch_slabs(chip).wait()

    unpack()
    count = samples.shape[2] // SUB

    def over_time(baseline):
        parts = []
        for part in range(2):
            parts.append(
                jnp.concatenate(
                    [samples[part, quad, pl.ds(baseline, count, stride=SUB), :] for quad in range(quads)], axis=1
                )
            )
        data = jnp.concatenate(parts, axis=0)
        high = data.astype(jnp.bfloat16)
        low = (data - high.astype(jnp.float32)).astype(jnp.bfloat16)
        for chip in range(len(fringe_refs)):
            for core in range(CORES):
                mats[place_ref[0] ^ (chip * CORES + core)] = slabs[chip, core, baseline]
        whole = mats[...].reshape(2 * count, count)
        real, imag = whole[:count], whole[count:]
        both = jnp.concatenate(
            [jnp.concatenate([real, -imag], axis=1), jnp.concatenate([imag, real], axis=1)], axis=0
        )
        rated = jnp.dot(both, high, preferred_element_type=jnp.float32) + jnp.dot(
            both, low, preferred_element_type=jnp.float32
        )
        high = rated.astype(jnp.bfloat16)
        low = (rated - high.astype(jnp.float32)).astype(jnp.bfloat16)
        return jnp.concatenate([high, low], axis=0)

    def over_channels(baseline, both):
        slot = baseline % results.shape[0]
        wide = delay.shape[3]
        for piece in range(delay.shape[1]):
            fetch_delay(baseline, piece).wait()
        if baseline >= results.shape[0]:
            for part in range(2):
                send_out(baseline, slot, part).wait()
        for part in range(2):
            rowsel = jnp.concatenate(
                [both[part * count : (part + 1) * count], both[(2 + part) * count : (3 + part) * count]], axis=0
            )
            total = None
            for piece in range(delay.shape[1]):
                term = lax.dot_general(
                    rowsel[:, piece * wide : (piece + 1) * wide],
                    delay[baseline, piece],
                    (((1,), (1,)), ((), ())),
                    preferred_element_type=jnp.float32,
                )
                total = term if total is None else total + term
            results[slot, part] = total[:count] + total[count:]
            send_out(baseline, slot, part).start()

    ready = over_time(0)
    for baseline in range(baselines):
        following = over_time(baseline + 1) if baseline + 1 < baselines else None
        over_channels(baseline, ready)
        ready = following
    for baseline in range(baselines - results.shape[0], baselines):
        for part in range(2):
            send_out(baseline, baseline % results.shape[0], part).wait()


def shards(visibility, groups, flags, fringe, delay):
    time_count = lax.axis_size("tm")
    chan_count = lax.axis_size("chan")
    everyone = ("tm", "chan")
    devices = time_count * chan_count
    total = groups.shape[0]
    own = total // devices
    times, chans = visibility.shape[2], visibility.shape[3]
    all_times, all_chans = times * time_count, chans * chan_count
    time_place = lax.axis_index("tm")
    chan_place = lax.axis_index("chan")
    place = jnp.stack([time_place, chan_place]).astype(jnp.int32)
    params = functools.partial(pltpu.CompilerParams, vmem_limit_bytes=VMEM)

    delay_groups = delay.shape[0]
    pieces = time_count // delay_groups
    wide = all_chans // pieces
    share = lax.dynamic_slice(
        delay, (time_place // pieces, 0, (time_place % pieces) * wide), (1, chans, wide)
    )
    share = lax.all_to_all(
        jnp.broadcast_to(share, (chan_count, chans, wide)), "chan", split_axis=0, concat_axis=0, tiled=True
    )

    rows = times * chans * SUB // LANES // SUB * own + 1
    step_lanes = 2 * LANES
    steps = total // step_lanes
    far = pl.BlockSpec(memory_space=pltpu.HBM)
    packed = pl.pallas_call(
        functools.partial(pack_kernel, rows=rows),
        in_specs=[far, far],
        out_specs=far,
        scratch_shapes=[
            pltpu.VMEM((steps, 2, times, chans, step_lanes), jnp.float32),
            pltpu.VMEM((chans, total), jnp.int32),
            pltpu.VMEM((steps, step_lanes // SUB * rows, LANES), jnp.int32),
            pltpu.SemaphoreType.DMA((steps,)),
            pltpu.SemaphoreType.DMA,
            pltpu.SemaphoreType.DMA((steps,)),
        ],
        out_shape=jax.ShapeDtypeStruct((devices * rows, LANES), jnp.int32),
        compiler_params=pltpu.CompilerParams(vmem_limit_bytes=LARGE_VMEM),
        name="pack",
    )(jnp.transpose(visibility, (0, 2, 3, 1)), flags.T)
    share, fringe, packed = lax.optimization_barrier((share, fringe, packed))
    delay_all = lax.all_gather(share.reshape(all_chans, wide), "tm", axis=0, tiled=True)
    delay_all = delay_all.reshape(delay_groups, pieces, all_chans, wide)
    words = lax.all_to_all(
        packed.reshape(devices, 1, rows * LANES), everyone, split_axis=0, concat_axis=0, tiled=True
    )
    words = words.reshape(time_count, chan_count * rows, LANES)

    def crossed(array, mask):
        return lax.ppermute(array, "tm", [(k, k ^ mask) for k in range(time_count)]) if mask else array

    chips = time_count // CORES
    held = fringe.shape[1]
    slab = 2 * all_times // time_count
    inside = pl.BlockSpec(memory_space=pltpu.VMEM)

    def exchanged(arrays):
        _, *block = arrays[0].shape
        turned = pl.pallas_call(
            regroup_kernel,
            in_specs=[inside] * CORES,
            out_specs=[inside] * chips,
            out_shape=[jax.ShapeDtypeStruct((CORES, *block), jnp.bfloat16)] * chips,
            compiler_params=params(),
            name="regroup",
        )(*[crossed(array, core) for core, array in enumerate(arrays)])
        return [crossed(array, chip * CORES) for chip, array in enumerate(turned)]

    shares = pl.pallas_call(
        shares_kernel,
        grid_spec=pltpu.PrefetchScalarGridSpec(
            num_scalar_prefetch=1, grid=(), in_specs=[inside], out_specs=[inside] * CORES
        ),
        out_shape=[jax.ShapeDtypeStruct((chips, held, slab, all_times), jnp.bfloat16)] * CORES,
        compiler_params=params(),
        name="shares",
    )(place, fringe.reshape(2, held, all_times // slab, slab, all_times))
    chosen = pl.pallas_call(
        select_kernel,
        grid_spec=pltpu.PrefetchScalarGridSpec(
            num_scalar_prefetch=2,
            grid=(),
            in_specs=[inside] * chips,
            out_specs=[inside] * CORES,
            scratch_shapes=[pltpu.VMEM((time_count, held, slab, all_times), jnp.bfloat16)],
        ),
        out_shape=[jax.ShapeDtypeStruct((chips, own, slab, all_times), jnp.bfloat16)] * CORES,
        compiler_params=params(),
        name="select",
    )(groups, place, *exchanged(shares))
    mats = exchanged(chosen)

    spread = time_count * held // delay_groups

    return pl.pallas_call(
        functools.partial(filter_kernel, rows=rows, spread=spread),
        grid_spec=pltpu.PrefetchScalarGridSpec(
            num_scalar_prefetch=2,
            grid=(),
            in_specs=[pl.BlockSpec(memory_space=pltpu.HBM)] * 2 + [pl.BlockSpec(memory_space=pl.ANY)] * chips,
            out_specs=pl.BlockSpec(memory_space=pl.ANY),
            scratch_shapes=[
                pltpu.VMEM((time_count, chan_count * rows, LANES), jnp.int32),
                pltpu.VMEM((LANES, LANES), jnp.float32),
                pltpu.VMEM((2, all_chans // LANES, all_times * SUB, LANES), jnp.float32),
                pltpu.VMEM((chips, CORES, own, slab, all_times), jnp.bfloat16),
                pltpu.VMEM((time_count, slab, all_times), jnp.bfloat16),
                pltpu.VMEM((own, pieces, all_chans, wide), jnp.bfloat16),
                pltpu.VMEM((4, 2, all_times, all_chans), jnp.float32),
                pltpu.SemaphoreType.DMA((time_count,)),
                pltpu.SemaphoreType.DMA((chips,)),
                pltpu.SemaphoreType.DMA((own, pieces)),
                pltpu.SemaphoreType.DMA((4, 2)),
            ],
        ),
        out_shape=jax.ShapeDtypeStruct((2, own, all_times, all_chans), jnp.float32),
        compiler_params=pltpu.CompilerParams(vmem_limit_bytes=LARGE_VMEM),
        name="filter",
    )(groups, place, words, delay_all, *mats)


def solution(mesh):
    placed = (
        P(None, None, "tm", "chan"),
        P(),
        P(None, "chan"),
        P(None, "tm", None, None),
        P(None, "chan", None),
    )
    return jax.shard_map(
        shards,
        mesh=mesh,
        in_specs=placed,
        out_specs=P(None, ("tm", "chan"), None, None),
        check_vma=False,
    )
```

```python
import functools

import jax
import jax.numpy as jnp
from jax import lax
from jax.experimental import pallas as pl
from jax.experimental.pallas import tpu as pltpu
from jax.sharding import PartitionSpec as P

LANES = 128
SUB = 8
FULL = 32760.0
MIDDLE = 32768.0
VMEM = 32 * 1024 * 1024
LARGE_VMEM = 60 * 1024 * 1024
CORES = 2


def pack_kernel(vis_ref, flag_ref, out_ref, vis, flag, packed, vis_sems, flag_sem, out_sems, *, rows):
    steps, lanes = vis.shape[0], vis.shape[4]
    owners = LANES // SUB

    def fetch_vis(step):
        there = pl.ds(pl.multiple_of(step * lanes, lanes), lanes)
        return pltpu.make_async_copy(vis_ref.at[:, :, :, there], vis.at[step], vis_sems.at[step])

    def fetch_flag():
        return pltpu.make_async_copy(flag_ref, flag, flag_sem)

    def send_out(step):
        there = pl.ds(pl.multiple_of(step * packed.shape[1], SUB), packed.shape[1])
        return pltpu.make_async_copy(packed.at[step], out_ref.at[there], out_sems.at[step])

    fetch_flag().start()
    for step in range(steps):
        fetch_vis(step).start()
    fetch_flag().wait()

    def one(step, carry):
        fetch_vis(step).wait()
        for tile in range(lanes // LANES):
            here = pl.ds(tile * LANES, LANES)
            keep = flag[:, pl.ds(pl.multiple_of(step * lanes + tile * LANES, LANES), LANES)].astype(jnp.float32)
            masked = vis[step, :, :, :, here] * keep[None, None]
            loudest = jnp.max(jnp.abs(masked), axis=(0, 1, 2), keepdims=True)
            level = jnp.ceil(jnp.log2(jnp.maximum(loudest, 1e-30)) * 4.0)
            factor = FULL / jnp.exp2(level * 0.25)
            coded = (masked * factor + (MIDDLE + 0.5)).astype(jnp.int32)
            words = coded[0] | (coded[1] << 16)
            level_row = level.reshape(1, LANES).astype(jnp.int32)
            times, chans = words.shape[0], words.shape[1]
            fold = LANES // chans
            for part in range(times // fold):
                turned = words[part * fold : (part + 1) * fold].reshape(LANES, LANES).T
                for owner in range(owners):
                    place = (tile * owners + owner) * rows + part * SUB
                    packed[step, place : place + SUB, :] = turned[owner * SUB : (owner + 1) * SUB]
            for owner in range(owners):
                place = (tile * owners + owner) * rows + rows - 1
                packed[step, place : place + 1, :] = level_row
        send_out(step).start()
        return carry

    lax.fori_loop(0, steps, one, 0)
    for step in range(steps):
        send_out(step).wait()


def shares_kernel(place_ref, fringe_ref, *out_refs):
    halves, pieces = fringe_ref.shape[0], fringe_ref.shape[2]
    for core, out_ref in enumerate(out_refs):
        for chip in range(out_ref.shape[0]):
            slab = place_ref[0] ^ (chip * CORES + core)
            out_ref[chip] = fringe_ref[slab // pieces, :, lax.rem(slab, pieces)]


def regroup_kernel(*refs):
    for core in range(CORES):
        for chip, out_ref in enumerate(refs[CORES:]):
            out_ref[core] = refs[core][chip]


def select_kernel(groups_ref, place_ref, *refs):
    in_refs, out_refs, table = refs[: -CORES - 1], refs[-CORES - 1 : -1], refs[-1]
    count, held, each = table.shape[0], table.shape[1], out_refs[0].shape[1]
    chan_count = groups_ref.shape[0] // (count * each)
    for chip, in_ref in enumerate(in_refs):
        for core in range(CORES):
            table[place_ref[0] ^ (chip * CORES + core)] = in_ref[core]
    for core, out_ref in enumerate(out_refs):
        for chip in range(out_ref.shape[0]):
            owner = place_ref[0] ^ (chip * CORES + core)
            for slot in range(each):
                group = groups_ref[(owner * chan_count + place_ref[1]) * each + slot]
                out_ref[chip, slot] = table[group // held, lax.rem(group, held)]


def filter_kernel(groups_ref, place_ref, words_ref, delay_ref, *refs, rows, spread):
    fringe_refs = refs[:-12]
    out_ref, words, levels, samples, slabs, mats, delay, results, *sems = refs[-12:]
    word_sems, slab_sems, delay_sems, out_sems = sems
    baselines = delay.shape[0]
    blocks = words_ref.shape[0]
    chan_count = words_ref.shape[1] // rows
    quads = chan_count // 4

    def fetch_words(block):
        there = words.at[block, pl.ds(0, words_ref.shape[1])]
        return pltpu.make_async_copy(words_ref.at[block], there, word_sems.at[block])

    def fetch_slabs(chip):
        return pltpu.make_async_copy(fringe_refs[chip], slabs.at[chip], slab_sems.at[chip])

    def fetch_delay(baseline, piece):
        mine = (place_ref[0] * chan_count + place_ref[1]) * baselines + baseline
        group = groups_ref[mine] // spread
        return pltpu.make_async_copy(
            delay_ref.at[group, piece], delay.at[baseline, piece], delay_sems.at[baseline, piece]
        )

    def send_out(baseline, slot, part):
        return pltpu.make_async_copy(
            results.at[slot, part], out_ref.at[part, baseline], out_sems.at[slot, part]
        )

    def unpack():
        for block in range(blocks):
            fetch_words(block).start()
        for chip in range(len(fringe_refs)):
            fetch_slabs(chip).start()
        lane = lax.broadcasted_iota(jnp.int32, (SUB, LANES), 1)
        low_half = lane < 64
        even_group = (lane & 32) == 0
        group = lane // 32
        def unpack_block(block, carry):
            fetch_words(block).wait()
            fetch_delay(block // delay.shape[1], lax.rem(block, delay.shape[1])).start()
            level = words[block, pl.ds(rows - 1, chan_count, stride=rows), :].astype(jnp.float32)
            scales = jnp.exp2(level * 0.25) * (1.0 / FULL)
            scales = jnp.concatenate([scales, jnp.zeros((LANES - chan_count, LANES), jnp.float32)], axis=0)
            levels[...] = scales.T
            own = levels[pl.ds(pl.multiple_of(place_ref[1] * SUB, SUB), SUB), :]
            for quad in range(quads):
                first = quad * 4
                scale = jnp.broadcast_to(own[:, first : first + 1], (SUB, LANES))
                for member in range(1, 4):
                    other = jnp.broadcast_to(own[:, first + member : first + member + 1], (SUB, LANES))
                    scale = jnp.where(group == member, other, scale)
                offset = scale * -MIDDLE
                for half in range((rows - 1) // SUB):
                    v = [
                        words[block, pl.ds((quad * 4 + member) * rows + half * SUB, SUB), :]
                        for member in range(4)
                    ]
                    r = [pltpu.roll(x, 64, 1) for x in v]
                    a0 = jnp.where(low_half, v[0], r[2])
                    a2 = jnp.where(low_half, r[0], v[2])
                    a1 = jnp.where(low_half, v[1], r[3])
                    a3 = jnp.where(low_half, r[1], v[3])
                    turned = (
                        jnp.where(even_group, a0, pltpu.roll(a1, 32, 1)),
                        jnp.where(even_group, pltpu.roll(a0, 96, 1), a1),
                        jnp.where(even_group, a2, pltpu.roll(a3, 32, 1)),
                        jnp.where(even_group, pltpu.roll(a2, 96, 1), a3),
                    )
                    for step, word in enumerate(turned):
                        at = pl.ds(pl.multiple_of((block * 8 + half * 4 + step) * SUB, SUB), SUB)
                        real = (word & 0xFFFF).astype(jnp.float32) * scale + offset
                        imag = lax.shift_right_logical(word, 16).astype(jnp.float32) * scale + offset
                        samples[0, quad, at, :] = real
                        samples[1, quad, at, :] = imag
            return carry

        lax.fori_loop(0, blocks, unpack_block, 0)
        for chip in range(len(fringe_refs)):
            fetch_slabs(chip).wait()

    unpack()
    count = results.shape[2]

    def over_time(baseline):
        parts = []
        for part in range(2):
            parts.append(
                jnp.concatenate(
                    [samples[part, quad, pl.ds(baseline, count, stride=SUB), :] for quad in range(quads)], axis=1
                )
            )
        data = jnp.concatenate(parts, axis=0)
        high = data.astype(jnp.bfloat16)
        low = (data - high.astype(jnp.float32)).astype(jnp.bfloat16)
        for chip in range(len(fringe_refs)):
            for core in range(CORES):
                mats[place_ref[0] ^ (chip * CORES + core)] = slabs[chip, core, baseline]
        whole = mats[...].reshape(2 * count, count)
        real, imag = whole[:count], whole[count:]
        both = jnp.concatenate(
            [jnp.concatenate([real, -imag], axis=1), jnp.concatenate([imag, real], axis=1)], axis=0
        )
        rated = jnp.dot(both, high, preferred_element_type=jnp.float32) + jnp.dot(
            both, low, preferred_element_type=jnp.float32
        )
        high = rated.astype(jnp.bfloat16)
        low = (rated - high.astype(jnp.float32)).astype(jnp.bfloat16)
        return jnp.concatenate([high, low], axis=0)

    def over_channels(baseline, both):
        slot = baseline % results.shape[0]
        wide = delay.shape[3]
        for piece in range(delay.shape[1]):
            fetch_delay(baseline, piece).wait()
        if baseline >= results.shape[0]:
            for part in range(2):
                send_out(baseline, slot, part).wait()
        for part in range(2):
            rowsel = jnp.concatenate(
                [both[part * count : (part + 1) * count], both[(2 + part) * count : (3 + part) * count]], axis=0
            )
            total = None
            for piece in range(delay.shape[1]):
                term = lax.dot_general(
                    rowsel[:, piece * wide : (piece + 1) * wide],
                    delay[baseline, piece],
                    (((1,), (1,)), ((), ())),
                    preferred_element_type=jnp.float32,
                )
                total = term if total is None else total + term
            results[slot, part] = total[:count] + total[count:]
            send_out(baseline, slot, part).start()

    ready = over_time(0)
    for baseline in range(baselines):
        following = over_time(baseline + 1) if baseline + 1 < baselines else None
        over_channels(baseline, ready)
        ready = following
    for baseline in range(baselines - results.shape[0], baselines):
        for part in range(2):
            send_out(baseline, baseline % results.shape[0], part).wait()


def shards(visibility, groups, flags, fringe, delay):
    time_count = lax.axis_size("tm")
    chan_count = lax.axis_size("chan")
    everyone = ("tm", "chan")
    devices = time_count * chan_count
    total = groups.shape[0]
    own = total // devices
    times, chans = visibility.shape[2], visibility.shape[3]
    all_times, all_chans = times * time_count, chans * chan_count
    time_place = lax.axis_index("tm")
    chan_place = lax.axis_index("chan")
    place = jnp.stack([time_place, chan_place]).astype(jnp.int32)
    params = functools.partial(pltpu.CompilerParams, vmem_limit_bytes=VMEM)

    delay_groups = delay.shape[0]
    pieces = time_count // delay_groups
    wide = all_chans // pieces
    share = lax.dynamic_slice(
        delay, (time_place // pieces, 0, (time_place % pieces) * wide), (1, chans, wide)
    )
    share = lax.all_to_all(
        jnp.broadcast_to(share, (chan_count, chans, wide)), "chan", split_axis=0, concat_axis=0, tiled=True
    )

    rows = times * chans * SUB // LANES // SUB * own + 1
    step_lanes = 2 * LANES
    steps = total // step_lanes
    far = pl.BlockSpec(memory_space=pltpu.HBM)
    packed = pl.pallas_call(
        functools.partial(pack_kernel, rows=rows),
        in_specs=[far, far],
        out_specs=far,
        scratch_shapes=[
            pltpu.VMEM((steps, 2, times, chans, step_lanes), jnp.float32),
            pltpu.VMEM((chans, total), jnp.int32),
            pltpu.VMEM((steps, step_lanes // SUB * rows, LANES), jnp.int32),
            pltpu.SemaphoreType.DMA((steps,)),
            pltpu.SemaphoreType.DMA,
            pltpu.SemaphoreType.DMA((steps,)),
        ],
        out_shape=jax.ShapeDtypeStruct((devices * rows, LANES), jnp.int32),
        compiler_params=pltpu.CompilerParams(vmem_limit_bytes=LARGE_VMEM),
        name="pack",
    )(jnp.transpose(visibility, (0, 2, 3, 1)), flags.T)
    share, fringe, packed = lax.optimization_barrier((share, fringe, packed))
    delay_all = lax.all_gather(share.reshape(all_chans, wide), "tm", axis=0, tiled=True)
    delay_all = delay_all.reshape(delay_groups, pieces, all_chans, wide)
    words = lax.all_to_all(
        packed.reshape(devices, 1, rows * LANES), everyone, split_axis=0, concat_axis=0, tiled=True
    )
    words = words.reshape(time_count, chan_count * rows, LANES)

    def crossed(array, mask):
        return lax.ppermute(array, "tm", [(k, k ^ mask) for k in range(time_count)]) if mask else array

    chips = time_count // CORES
    held = fringe.shape[1]
    slab = 2 * all_times // time_count
    inside = pl.BlockSpec(memory_space=pltpu.VMEM)

    def exchanged(arrays):
        _, *block = arrays[0].shape
        turned = pl.pallas_call(
            regroup_kernel,
            in_specs=[inside] * CORES,
            out_specs=[inside] * chips,
            out_shape=[jax.ShapeDtypeStruct((CORES, *block), jnp.bfloat16)] * chips,
            compiler_params=params(),
            name="regroup",
        )(*[crossed(array, core) for core, array in enumerate(arrays)])
        return [crossed(array, chip * CORES) for chip, array in enumerate(turned)]

    shares = pl.pallas_call(
        shares_kernel,
        grid_spec=pltpu.PrefetchScalarGridSpec(
            num_scalar_prefetch=1, grid=(), in_specs=[inside], out_specs=[inside] * CORES
        ),
        out_shape=[jax.ShapeDtypeStruct((chips, held, slab, all_times), jnp.bfloat16)] * CORES,
        compiler_params=params(),
        name="shares",
    )(place, fringe.reshape(2, held, all_times // slab, slab, all_times))
    chosen = pl.pallas_call(
        select_kernel,
        grid_spec=pltpu.PrefetchScalarGridSpec(
            num_scalar_prefetch=2,
            grid=(),
            in_specs=[inside] * chips,
            out_specs=[inside] * CORES,
            scratch_shapes=[pltpu.VMEM((time_count, held, slab, all_times), jnp.bfloat16)],
        ),
        out_shape=[jax.ShapeDtypeStruct((chips, own, slab, all_times), jnp.bfloat16)] * CORES,
        compiler_params=params(),
        name="select",
    )(groups, place, *exchanged(shares))
    mats = exchanged(chosen)

    spread = time_count * held // delay_groups

    return pl.pallas_call(
        functools.partial(filter_kernel, rows=rows, spread=spread),
        grid_spec=pltpu.PrefetchScalarGridSpec(
            num_scalar_prefetch=2,
            grid=(),
            in_specs=[pl.BlockSpec(memory_space=pltpu.HBM)] * 2 + [pl.BlockSpec(memory_space=pl.ANY)] * chips,
            out_specs=pl.BlockSpec(memory_space=pl.ANY),
            scratch_shapes=[
                pltpu.VMEM((time_count, chan_count * rows + LANES // SUB, LANES), jnp.int32),
                pltpu.VMEM((LANES, LANES), jnp.float32),
                pltpu.VMEM((2, all_chans // LANES, all_times * SUB + SUB, LANES), jnp.float32),
                pltpu.VMEM((chips, CORES, own, slab, all_times), jnp.bfloat16),
                pltpu.VMEM((time_count, slab, all_times), jnp.bfloat16),
                pltpu.VMEM((own, pieces, all_chans, wide), jnp.bfloat16),
                pltpu.VMEM((4, 2, all_times, all_chans), jnp.float32),
                pltpu.SemaphoreType.DMA((time_count,)),
                pltpu.SemaphoreType.DMA((chips,)),
                pltpu.SemaphoreType.DMA((own, pieces)),
                pltpu.SemaphoreType.DMA((4, 2)),
            ],
        ),
        out_shape=jax.ShapeDtypeStruct((2, own, all_times, all_chans), jnp.float32),
        compiler_params=pltpu.CompilerParams(vmem_limit_bytes=LARGE_VMEM),
        name="filter",
    )(groups, place, words, delay_all, *mats)


def solution(mesh):
    placed = (
        P(None, None, "tm", "chan"),
        P(),
        P(None, "chan"),
        P(None, "tm", None, None),
        P(None, "chan", None),
    )
    return jax.shard_map(
        shards,
        mesh=mesh,
        in_specs=placed,
        out_specs=P(None, ("tm", "chan"), None, None),
        check_vma=False,
    )
```

```python
import functools

import jax
import jax.numpy as jnp
from jax import lax
from jax.experimental import pallas as pl
from jax.experimental.pallas import tpu as pltpu
from jax.sharding import PartitionSpec as P

LANES = 128
SUB = 8
FULL = 32760.0
MIDDLE = 32768.0
VMEM = 32 * 1024 * 1024
LARGE_VMEM = 60 * 1024 * 1024
PACK_VMEM = 64 * 1024 * 1024 - 128 * 1024
CORES = 2


def pack_kernel(vis_ref, flag_ref, out_ref, vis, flag, packed, vis_sems, flag_sem, out_sems, *, rows):
    steps, lanes = vis.shape[0], vis.shape[4]
    owners = LANES // SUB

    def fetch_vis(step):
        there = pl.ds(pl.multiple_of(step * lanes, lanes), lanes)
        return pltpu.make_async_copy(vis_ref.at[:, :, :, there], vis.at[step], vis_sems.at[step])

    def fetch_flag():
        return pltpu.make_async_copy(flag_ref, flag, flag_sem)

    def send_out(step):
        there = pl.ds(pl.multiple_of(step * packed.shape[1], SUB), packed.shape[1])
        return pltpu.make_async_copy(packed.at[step], out_ref.at[there], out_sems.at[step])

    fetch_flag().start()
    for step in range(steps):
        fetch_vis(step).start()
    fetch_flag().wait()

    def one(step, carry):
        fetch_vis(step).wait()
        for tile in range(lanes // LANES):
            here = pl.ds(tile * LANES, LANES)
            keep = flag[:, pl.ds(pl.multiple_of(step * lanes + tile * LANES, LANES), LANES)].astype(jnp.float32)
            masked = vis[step, :, :, :, here] * keep[None, None]
            loudest = jnp.max(jnp.abs(masked), axis=(0, 1, 2), keepdims=True)
            level = jnp.ceil(jnp.log2(jnp.maximum(loudest, 1e-30)) * 4.0)
            factor = FULL / jnp.exp2(level * 0.25)
            coded = (masked * factor + (MIDDLE + 0.5)).astype(jnp.int32)
            words = coded[0] | (coded[1] << 16)
            level_row = level.reshape(1, LANES).astype(jnp.int32)
            times, chans = words.shape[0], words.shape[1]
            fold = LANES // chans
            for part in range(times // fold):
                turned = words[part * fold : (part + 1) * fold].reshape(LANES, LANES).T
                for owner in range(owners):
                    place = (tile * owners + owner) * rows + part * SUB
                    packed[step, place : place + SUB, :] = turned[owner * SUB : (owner + 1) * SUB]
            for owner in range(owners):
                place = (tile * owners + owner) * rows + rows - 1
                packed[step, place : place + 1, :] = level_row
        send_out(step).start()
        return carry

    lax.fori_loop(0, steps, one, 0)
    for step in range(steps):
        send_out(step).wait()


def shares_kernel(place_ref, fringe_ref, *out_refs):
    halves, pieces = fringe_ref.shape[0], fringe_ref.shape[2]
    for core, out_ref in enumerate(out_refs):
        for chip in range(out_ref.shape[0]):
            slab = place_ref[0] ^ (chip * CORES + core)
            out_ref[chip] = fringe_ref[slab // pieces, :, lax.rem(slab, pieces)]


def regroup_kernel(*refs):
    for core in range(CORES):
        for chip, out_ref in enumerate(refs[CORES:]):
            out_ref[core] = refs[core][chip]


def select_kernel(groups_ref, place_ref, *refs):
    in_refs, out_refs, table = refs[: -CORES - 1], refs[-CORES - 1 : -1], refs[-1]
    count, held, each = table.shape[0], table.shape[1], out_refs[0].shape[1]
    chan_count = groups_ref.shape[0] // (count * each)
    for chip, in_ref in enumerate(in_refs):
        for core in range(CORES):
            table[place_ref[0] ^ (chip * CORES + core)] = in_ref[core]
    for core, out_ref in enumerate(out_refs):
        for chip in range(out_ref.shape[0]):
            owner = place_ref[0] ^ (chip * CORES + core)
            for slot in range(each):
                group = groups_ref[(owner * chan_count + place_ref[1]) * each + slot]
                out_ref[chip, slot] = table[group // held, lax.rem(group, held)]


def filter_kernel(groups_ref, place_ref, words_ref, delay_ref, *refs, rows, spread):
    fringe_refs = refs[:-12]
    out_ref, words, levels, samples, slabs, mats, delay, results, *sems = refs[-12:]
    word_sems, slab_sems, delay_sems, out_sems = sems
    baselines = delay.shape[0]
    blocks = words_ref.shape[0]
    chan_count = words_ref.shape[1] // rows
    quads = chan_count // 4

    def fetch_words(block):
        there = words.at[block, pl.ds(0, words_ref.shape[1])]
        return pltpu.make_async_copy(words_ref.at[block], there, word_sems.at[block])

    def fetch_slabs(chip):
        return pltpu.make_async_copy(fringe_refs[chip], slabs.at[chip], slab_sems.at[chip])

    def fetch_delay(baseline, piece):
        mine = (place_ref[0] * chan_count + place_ref[1]) * baselines + baseline
        group = groups_ref[mine] // spread
        return pltpu.make_async_copy(
            delay_ref.at[group, piece], delay.at[baseline, piece], delay_sems.at[baseline, piece]
        )

    def send_out(baseline, slot, part):
        return pltpu.make_async_copy(
            results.at[slot, part], out_ref.at[part, baseline], out_sems.at[slot, part]
        )

    def unpack():
        for block in range(blocks):
            fetch_words(block).start()
        for chip in range(len(fringe_refs)):
            fetch_slabs(chip).start()
        lane = lax.broadcasted_iota(jnp.int32, (SUB, LANES), 1)
        low_half = lane < 64
        even_group = (lane & 32) == 0
        group = lane // 32
        def unpack_block(block, carry):
            fetch_words(block).wait()
            fetch_delay(block // delay.shape[1], lax.rem(block, delay.shape[1])).start()
            level = words[block, pl.ds(rows - 1, chan_count, stride=rows), :].astype(jnp.float32)
            scales = jnp.exp2(level * 0.25) * (1.0 / FULL)
            scales = jnp.concatenate([scales, jnp.zeros((LANES - chan_count, LANES), jnp.float32)], axis=0)
            levels[...] = scales.T
            own = levels[pl.ds(pl.multiple_of(place_ref[1] * SUB, SUB), SUB), :]
            for quad in range(quads):
                first = quad * 4
                scale = jnp.broadcast_to(own[:, first : first + 1], (SUB, LANES))
                for member in range(1, 4):
                    other = jnp.broadcast_to(own[:, first + member : first + member + 1], (SUB, LANES))
                    scale = jnp.where(group == member, other, scale)
                offset = scale * -MIDDLE
                for half in range((rows - 1) // SUB):
                    v = [
                        words[block, pl.ds((quad * 4 + member) * rows + half * SUB, SUB), :]
                        for member in range(4)
                    ]
                    r = [pltpu.roll(x, 64, 1) for x in v]
                    a0 = jnp.where(low_half, v[0], r[2])
                    a2 = jnp.where(low_half, r[0], v[2])
                    a1 = jnp.where(low_half, v[1], r[3])
                    a3 = jnp.where(low_half, r[1], v[3])
                    turned = (
                        jnp.where(even_group, a0, pltpu.roll(a1, 32, 1)),
                        jnp.where(even_group, pltpu.roll(a0, 96, 1), a1),
                        jnp.where(even_group, a2, pltpu.roll(a3, 32, 1)),
                        jnp.where(even_group, pltpu.roll(a2, 96, 1), a3),
                    )
                    for step, word in enumerate(turned):
                        at = pl.ds(pl.multiple_of((block * 8 + half * 4 + step) * SUB, SUB), SUB)
                        real = (word & 0xFFFF).astype(jnp.float32) * scale + offset
                        imag = lax.shift_right_logical(word, 16).astype(jnp.float32) * scale + offset
                        samples[0, quad, at, :] = real
                        samples[1, quad, at, :] = imag
            return carry

        lax.fori_loop(0, blocks, unpack_block, 0)
        for chip in range(len(fringe_refs)):
            fetch_slabs(chip).wait()

    unpack()
    count = results.shape[2]

    def over_time(baseline):
        parts = []
        for part in range(2):
            parts.append(
                jnp.concatenate(
                    [samples[part, quad, pl.ds(baseline, count, stride=SUB), :] for quad in range(quads)], axis=1
                )
            )
        data = jnp.concatenate(parts, axis=0)
        high = data.astype(jnp.bfloat16)
        low = (data - high.astype(jnp.float32)).astype(jnp.bfloat16)
        for chip in range(len(fringe_refs)):
            for core in range(CORES):
                mats[place_ref[0] ^ (chip * CORES + core)] = slabs[chip, core, baseline]
        whole = mats[...].reshape(2 * count, count)
        real, imag = whole[:count], whole[count:]
        both = jnp.concatenate(
            [jnp.concatenate([real, -imag], axis=1), jnp.concatenate([imag, real], axis=1)], axis=0
        )
        rated = jnp.dot(both, high, preferred_element_type=jnp.float32) + jnp.dot(
            both, low, preferred_element_type=jnp.float32
        )
        high = rated.astype(jnp.bfloat16)
        low = (rated - high.astype(jnp.float32)).astype(jnp.bfloat16)
        return jnp.concatenate([high, low], axis=0)

    def over_channels(baseline, both):
        slot = baseline % results.shape[0]
        wide = delay.shape[3]
        for piece in range(delay.shape[1]):
            fetch_delay(baseline, piece).wait()
        if baseline >= results.shape[0]:
            for part in range(2):
                send_out(baseline, slot, part).wait()
        for part in range(2):
            rowsel = jnp.concatenate(
                [both[part * count : (part + 1) * count], both[(2 + part) * count : (3 + part) * count]], axis=0
            )
            total = None
            for piece in range(delay.shape[1]):
                term = lax.dot_general(
                    rowsel[:, piece * wide : (piece + 1) * wide],
                    delay[baseline, piece],
                    (((1,), (1,)), ((), ())),
                    preferred_element_type=jnp.float32,
                )
                total = term if total is None else total + term
            results[slot, part] = total[:count] + total[count:]
            send_out(baseline, slot, part).start()

    ready = over_time(0)
    for baseline in range(baselines):
        following = over_time(baseline + 1) if baseline + 1 < baselines else None
        over_channels(baseline, ready)
        ready = following
    for baseline in range(baselines - results.shape[0], baselines):
        for part in range(2):
            send_out(baseline, baseline % results.shape[0], part).wait()


def shards(visibility, groups, flags, fringe, delay):
    time_count = lax.axis_size("tm")
    chan_count = lax.axis_size("chan")
    everyone = ("tm", "chan")
    devices = time_count * chan_count
    total = groups.shape[0]
    own = total // devices
    times, chans = visibility.shape[2], visibility.shape[3]
    all_times, all_chans = times * time_count, chans * chan_count
    time_place = lax.axis_index("tm")
    chan_place = lax.axis_index("chan")
    place = jnp.stack([time_place, chan_place]).astype(jnp.int32)
    params = functools.partial(pltpu.CompilerParams, vmem_limit_bytes=VMEM)

    delay_groups = delay.shape[0]
    pieces = time_count // delay_groups
    wide = all_chans // pieces
    share = lax.dynamic_slice(
        delay, (time_place // pieces, 0, (time_place % pieces) * wide), (1, chans, wide)
    )
    share = lax.all_to_all(
        jnp.broadcast_to(share, (chan_count, chans, wide)), "chan", split_axis=0, concat_axis=0, tiled=True
    )

    rows = times * chans * SUB // LANES // SUB * own + 1
    step_lanes = 2 * LANES
    steps = total // step_lanes
    far = pl.BlockSpec(memory_space=pltpu.HBM)
    packed = pl.pallas_call(
        functools.partial(pack_kernel, rows=rows),
        in_specs=[far, far],
        out_specs=far,
        scratch_shapes=[
            pltpu.VMEM((steps, 2, times, chans, step_lanes), jnp.float32),
            pltpu.VMEM((chans, total), jnp.int32),
            pltpu.VMEM((steps, step_lanes // SUB * rows, LANES), jnp.int32),
            pltpu.SemaphoreType.DMA((steps,)),
            pltpu.SemaphoreType.DMA,
            pltpu.SemaphoreType.DMA((steps,)),
        ],
        out_shape=jax.ShapeDtypeStruct((devices * rows, LANES), jnp.int32),
        compiler_params=pltpu.CompilerParams(vmem_limit_bytes=PACK_VMEM),
        name="pack",
    )(jnp.transpose(visibility, (0, 2, 3, 1)), flags.T)
    share, fringe, packed = lax.optimization_barrier((share, fringe, packed))
    delay_all = lax.all_gather(share.reshape(all_chans, wide), "tm", axis=0, tiled=True)
    delay_all = delay_all.reshape(delay_groups, pieces, all_chans, wide)
    words = lax.all_to_all(
        packed.reshape(devices, 1, rows * LANES), everyone, split_axis=0, concat_axis=0, tiled=True
    )
    words = words.reshape(time_count, chan_count * rows, LANES)

    def crossed(array, mask):
        return lax.ppermute(array, "tm", [(k, k ^ mask) for k in range(time_count)]) if mask else array

    chips = time_count // CORES
    held = fringe.shape[1]
    slab = 2 * all_times // time_count
    inside = pl.BlockSpec(memory_space=pltpu.VMEM)

    def exchanged(arrays):
        _, *block = arrays[0].shape
        turned = pl.pallas_call(
            regroup_kernel,
            in_specs=[inside] * CORES,
            out_specs=[inside] * chips,
            out_shape=[jax.ShapeDtypeStruct((CORES, *block), jnp.bfloat16)] * chips,
            compiler_params=params(),
            name="regroup",
        )(*[crossed(array, core) for core, array in enumerate(arrays)])
        return [crossed(array, chip * CORES) for chip, array in enumerate(turned)]

    shares = pl.pallas_call(
        shares_kernel,
        grid_spec=pltpu.PrefetchScalarGridSpec(
            num_scalar_prefetch=1, grid=(), in_specs=[inside], out_specs=[inside] * CORES
        ),
        out_shape=[jax.ShapeDtypeStruct((chips, held, slab, all_times), jnp.bfloat16)] * CORES,
        compiler_params=params(),
        name="shares",
    )(place, fringe.reshape(2, held, all_times // slab, slab, all_times))
    chosen = pl.pallas_call(
        select_kernel,
        grid_spec=pltpu.PrefetchScalarGridSpec(
            num_scalar_prefetch=2,
            grid=(),
            in_specs=[inside] * chips,
            out_specs=[inside] * CORES,
            scratch_shapes=[pltpu.VMEM((time_count, held, slab, all_times), jnp.bfloat16)],
        ),
        out_shape=[jax.ShapeDtypeStruct((chips, own, slab, all_times), jnp.bfloat16)] * CORES,
        compiler_params=params(),
        name="select",
    )(groups, place, *exchanged(shares))
    mats = exchanged(chosen)

    spread = time_count * held // delay_groups

    return pl.pallas_call(
        functools.partial(filter_kernel, rows=rows, spread=spread),
        grid_spec=pltpu.PrefetchScalarGridSpec(
            num_scalar_prefetch=2,
            grid=(),
            in_specs=[pl.BlockSpec(memory_space=pltpu.HBM)] * 2 + [pl.BlockSpec(memory_space=pl.ANY)] * chips,
            out_specs=pl.BlockSpec(memory_space=pl.ANY),
            scratch_shapes=[
                pltpu.VMEM((time_count, chan_count * rows + LANES // SUB, LANES), jnp.int32),
                pltpu.VMEM((LANES, LANES), jnp.float32),
                pltpu.VMEM((2, all_chans // LANES, all_times * SUB + SUB, LANES), jnp.float32),
                pltpu.VMEM((chips, CORES, own, slab, all_times), jnp.bfloat16),
                pltpu.VMEM((time_count, slab, all_times), jnp.bfloat16),
                pltpu.VMEM((own, pieces, all_chans, wide), jnp.bfloat16),
                pltpu.VMEM((4, 2, all_times, all_chans), jnp.float32),
                pltpu.SemaphoreType.DMA((time_count,)),
                pltpu.SemaphoreType.DMA((chips,)),
                pltpu.SemaphoreType.DMA((own, pieces)),
                pltpu.SemaphoreType.DMA((4, 2)),
            ],
        ),
        out_shape=jax.ShapeDtypeStruct((2, own, all_times, all_chans), jnp.float32),
        compiler_params=pltpu.CompilerParams(vmem_limit_bytes=LARGE_VMEM),
        name="filter",
    )(groups, place, words, delay_all, *mats)


def solution(mesh):
    placed = (
        P(None, None, "tm", "chan"),
        P(),
        P(None, "chan"),
        P(None, "tm", None, None),
        P(None, "chan", None),
    )
    return jax.shard_map(
        shards,
        mesh=mesh,
        in_specs=placed,
        out_specs=P(None, ("tm", "chan"), None, None),
        check_vma=False,
    )
```
